32 devices in a mesh: fsdp: 8 (over z, x), rep: 4 (over y, core).
Axes of the slice: x: 2, y: 2, z: 4, core: 2. Of those that a mesh axis runs over, the one named last changes fastest.
Arguments:
- layer_input: bfloat16 [32768, 768], P(('fsdp', 'rep')), may hold values from -6 to 6
- qkv_weight: bfloat16 [768, 2304], P('fsdp'), may hold values from -0.21875 to 0.21875
- attn_weight: bfloat16 [768, 768], P('fsdp'), may hold values from -1.75 to 1.75
- wide_weight: bfloat16 [768, 2304], P('fsdp'), may hold values from -0.21875 to 0.21875
- narrow_weight: bfloat16 [768, 1152], P('fsdp'), may hold values from -0.375 to 0.375
- first_gain: bfloat16 [768], P('fsdp'), may hold values from 0.099609375 to 1.8984375
- second_gain: bfloat16 [768], P('fsdp'), may hold values from 0.099609375 to 1.8984375
- out_grad: bfloat16 [32768, 768], P(('fsdp', 'rep')), may hold values from -12 to 12
- token_seg: int32 [32768], P(('fsdp', 'rep')), may hold values from 0 to 255, as said below
- token_live: int32 [32768], P(('fsdp', 'rep')), may hold values from 0 to 1, as said below
Outputs:
- layer_output: bfloat16 [32768, 768], P(('fsdp', 'rep'))
- input_grad: float32 [32768, 768], P(('fsdp', 'rep'))
- qkv_grad: float32 [768, 2304], P('fsdp')
- attn_grad: float32 [768, 768], P('fsdp')
- wide_grad: float32 [768, 2304], P('fsdp')
- narrow_grad: float32 [768, 1152], P('fsdp')
- first_grad: float32 [768], P('fsdp')
- second_grad: float32 [768], P('fsdp')
The draws below stay inside these ranges and needn't reach their ends.
Inputs may be any that keep to these rules, and one draw needn't show every extreme that they name: `token_seg`: numbers never fall along the slots; all slots of one number lie in one block of 1024 slots (one device's), and each number begins at a multiple of 128; every block begins a new number; the last tile of the last block begins a number of its own. `token_live`: within each number of token_seg the live slots come first and its first slot is live; in every draw one block of 1024 slots holds a single number with every slot live.
All inputs are finite; a program needn't handle non-finite values.
Results may differ from the reference program's by a relative error of at most 0.018.
Values may be sent and summed in bfloat16 or wider, within the bound.
A program may use at most 320 MiB of HBM per device.

```python
import math
import jax
import jax.numpy as jnp
from jax import lax

D = 768
FF = 1152
HDIM = 64
TILE = 128
TOK_DEV = 1024
TOKENS = 32768
N_FSDP = 8
N_REP = 4


def layout_draw(key):
    base = jax.random.fold_in(key, 7)
    key_star, key_used, key_cut, key_fill = jax.random.split(base, 4)
    buffers = TOKENS // TOK_DEV
    tiles = TOK_DEV // TILE
    chosen = jax.random.randint(key_star, (), 0, buffers - 1)
    is_star = (jnp.arange(buffers) == chosen)[:, None]
    is_last = (jnp.arange(buffers) == buffers - 1)[:, None]
    used = jax.random.randint(key_used, (buffers, 1), tiles - tiles // 2, tiles + 1)
    used = jnp.where(is_star | is_last, tiles, used)
    column = jnp.arange(tiles)[None, :]
    breaks = jax.random.randint(key_cut, (buffers, tiles), 0, 5) < 2
    breaks = breaks & (column < used) & jnp.logical_not(is_star) | (column == 0)
    breaks = breaks | is_last & (column == tiles - 1)
    start_col = lax.cummax(jnp.where(breaks, column, 0), axis=1)
    tile_seg = start_col + jnp.arange(buffers, dtype=jnp.int32)[:, None] * tiles
    following = jnp.concatenate([breaks[:, 1:], jnp.ones((buffers, 1), dtype=jnp.bool_)], axis=1)
    closing = (column < used) & ((column == used - 1) | following)
    partial_fill = jax.random.randint(key_fill, (buffers, tiles), 1, TILE + 1)
    counts = jnp.where(closing, partial_fill, TILE)
    counts = jnp.where(column >= used, 0, counts)
    counts = jnp.where(is_star, TILE, counts)
    seg_tokens = jnp.repeat(tile_seg, TILE, axis=1).reshape(-1).astype(jnp.int32)
    live_tokens = (jnp.arange(TILE)[None, None, :] < counts[:, :, None]).astype(jnp.int32).reshape(-1)
    return (seg_tokens, live_tokens)


def draw_token_seg(key, part):
    return layout_draw(key)[0]


def draw_token_live(key, part):
    return layout_draw(key)[1]


def with_spikes(array, rng, source, target, blocks, factor):
    def block_of(position):
        return (jnp.arange(array.shape[position]) // (array.shape[position] // blocks)).reshape((-1,) + (1,) * (array.ndim - 1 - position))

    first = jax.random.permutation(rng, blocks)[block_of(target)]
    second = (block_of(target) + blocks // 2) % blocks
    return jnp.where((block_of(source) == first) | (block_of(source) == second), factor * array, array)


def steps_of(key, dims, shards, least, largest):
    gain, own = 1.0, jax.random.fold_in(key, 6)
    for dim, parts in shards:
        draws = jnp.exp(jax.random.uniform(jax.random.fold_in(own, dim), (parts,), jnp.float32, least / len(shards), largest / len(shards)))
        gain = gain * jnp.repeat(draws, dims[dim] // parts).reshape([-1 if axis == dim else 1 for axis in range(len(dims))])
    return gain


def noise(key, dims, scale, reach, cuts=(), kind=jnp.bfloat16):
    array = scale * jax.random.normal(key, dims, jnp.float32)
    if cuts:
        array = array * steps_of(key, dims, cuts, -0.22, 0.18)
    return jnp.clip(array, -reach, reach).astype(kind)


def noise_with(rng, shape, scale, bound, shards, heavy, kind=jnp.bfloat16):
    entries = scale * jax.random.normal(rng, shape, jnp.float32)
    if shards:
        entries = entries * steps_of(rng, shape, shards, -0.22, 0.18)
    return jnp.clip(with_spikes(entries, jax.random.fold_in(rng, 3), *heavy), -bound, bound).astype(kind)


def setup_inputs(seed: int = 0) -> dict:
    splits = jax.random.split(jax.random.key(seed), 11)
    return {
        "layer_input": noise(splits[0], (TOKENS, D), 1.0, 6.0, ((0, 32),)),
        "qkv_weight": noise(splits[1], (D, 3 * D), D ** -0.5, 0.21875, ((0, 8),)),
        "attn_weight": noise(splits[2], (D, D), (D // 64) ** -0.5, 1.75, ((0, 8),)),
        "wide_weight": noise(splits[3], (D, 2 * FF), D ** -0.5, 0.21875, ((0, 8),)),
        "narrow_weight": noise(splits[4], (D, FF), (FF // 4) ** -0.5, 0.375, ((0, 8),)),
        "first_gain": jnp.clip(1.0 + 0.18 * jax.random.normal(splits[5], (D,), jnp.float32), 0.099609375, 1.8984375).astype(jnp.bfloat16),
        "second_gain": jnp.clip(1.0 + 0.18 * jax.random.normal(splits[6], (D,), jnp.float32), 0.099609375, 1.8984375).astype(jnp.bfloat16),
        "out_grad": noise_with(splits[7], (TOKENS, D), 1.0, 12.0, ((0, 32),), (0, 1, 32, 2.75)),
        "token_seg": draw_token_seg(jax.random.fold_in(splits[10], 71), 0),
        "token_live": draw_token_live(jax.random.fold_in(splits[10], 71), 0),
    }


rope_base = 160000.0
eps = 1e-05
masked_score = -1e+30
highest = lax.Precision.HIGHEST

@jax.custom_vjp
def low(v):
    return lax.optimization_barrier(v.astype(jnp.bfloat16)).astype(jnp.float32)

@jax.custom_vjp
def low_back(v):
    return v

def low_keep(v):
    return (low(v), None)

def low_pass(kept, grad):
    return (grad,)

def back_keep(v):
    return (v, None)

def back_low(kept, grad):
    return (low(grad),)
low.defvjp(low_keep, low_pass)
low_back.defvjp(back_keep, back_low)

def layer_norm(values, scales):
    center = values - lax.optimization_barrier(jnp.mean(values, axis=-1, keepdims=True))
    spread = lax.optimization_barrier(jnp.mean(center * center, axis=-1, keepdims=True))
    return center * lax.rsqrt(spread + eps) * scales

def rope_tables(seg_rows):
    length = seg_rows.shape[0]
    firsts = seg_rows[::TILE]
    before = lax.optimization_barrier(jnp.sum((firsts[None, :] < seg_rows[:, None]).astype(jnp.int32), axis=1))
    places = jnp.arange(length, dtype=jnp.int32) - TILE * before
    freq_index = jnp.arange(HDIM // 2, dtype=jnp.float32)
    inverse = jnp.exp(freq_index * (-2.0 * math.log(rope_base) / HDIM))
    angles = places.astype(jnp.float32)[:, None] * inverse[None, :]
    angles = jnp.concatenate([angles, angles], axis=1)
    return (jnp.cos(angles)[:, None, :], jnp.sin(angles)[:, None, :])

def rotate(values, cos_tab, sin_tab):
    half_dim = values.shape[-1] // 2
    turned = jnp.concatenate([-values[..., half_dim:], values[..., :half_dim]], axis=-1)
    return values * cos_tab + turned * sin_tab

def buffer_forward(params, rows_in, seg_rows, live_rows):
    qkv_w, attn_w, wide_w, narrow_w, gain_one, gain_two = params
    length = rows_in.shape[0]
    head_count = D // HDIM
    scaling = 1.0 / math.sqrt(HDIM)
    normed_one = low(layer_norm(rows_in, gain_one))
    packed = low_back(jnp.dot(normed_one, qkv_w, precision=highest))
    cos_tab, sin_tab = rope_tables(seg_rows)
    queries = low(rotate(packed[:, :D].reshape(length, head_count, HDIM), cos_tab, sin_tab))
    keyset = low(rotate(packed[:, D:2 * D].reshape(length, head_count, HDIM), cos_tab, sin_tab))
    valueset = low(packed[:, 2 * D:].reshape(length, head_count, HDIM))
    scores = low_back(jnp.einsum('qhd,khd->hqk', queries, keyset, precision=highest) * scaling)
    allowed = (seg_rows[:, None] == seg_rows[None, :]) & (live_rows[None, :] > 0)
    scores = jnp.where(allowed[None], scores, masked_score)
    weights_soft = low(jax.nn.softmax(scores, axis=-1))
    mixed_rows = low(low_back(jnp.einsum('hqk,khd->qhd', weights_soft, valueset, precision=highest).reshape(length, D)))
    middle = rows_in + low_back(jnp.dot(mixed_rows, attn_w, precision=highest))
    normed_two = low(layer_norm(middle, gain_two))
    lifted = low_back(jnp.dot(normed_two, wide_w, precision=highest))
    hidden = low(jax.nn.gelu(lifted[:, :FF], approximate=False) * lifted[:, FF:])
    return middle + low_back(jnp.einsum('tf,df->td', hidden, narrow_w, precision=highest))

def reference(layer_input, qkv_weight, attn_weight, wide_weight, narrow_weight, first_gain, second_gain, out_grad, token_seg, token_live):
    buffers = N_FSDP * N_REP
    inputs_f32 = layer_input.astype(jnp.float32)
    params = tuple((matrix.astype(jnp.float32) for matrix in (qkv_weight, attn_weight, wide_weight, narrow_weight, first_gain, second_gain)))
    seg_blocks = token_seg.reshape(buffers, TOK_DEV)
    live_blocks = token_live.reshape(buffers, TOK_DEV)
    step_fn = jax.checkpoint(buffer_forward)

    def whole(values, weights_all):
        blocks = values.reshape(buffers, TOK_DEV, D)
        outputs = lax.map(lambda triple: step_fn(weights_all, triple[0], triple[1], triple[2]), (blocks, seg_blocks, live_blocks))
        return outputs.reshape(buffers * TOK_DEV, D)
    result, pullback = jax.vjp(whole, inputs_f32, params)
    cotangent = out_grad.astype(jnp.float32) * token_live.astype(jnp.float32)[:, None]
    input_grad, grads = pullback(cotangent)
    return (result.astype(jnp.bfloat16), input_grad, grads[0], grads[1], grads[2], grads[3], grads[4], grads[5])
```

```python
import math

import jax
import jax.numpy as jnp
from jax import lax
from jax.experimental import pallas as pl
from jax.experimental.pallas import tpu as pltpu
from jax.sharding import PartitionSpec as P

HDIM = 64
TILE = 128
PAIR = 128
QROWS = 256


rope_base = 160000.0
eps = 1e-05
masked_score = -1e30


def layer_norm(values, scales):
    center = values - jnp.mean(values, axis=-1, keepdims=True)
    spread = jnp.mean(center * center, axis=-1, keepdims=True)
    return center * lax.rsqrt(spread + eps) * scales


def rope_tables(seg_rows):
    length = seg_rows.shape[0]
    firsts = seg_rows[::TILE]
    before = jnp.sum((firsts[None, :] < seg_rows[:, None]).astype(jnp.int32), axis=1)
    places = jnp.arange(length, dtype=jnp.int32) - TILE * before
    freq_index = jnp.arange(HDIM // 2, dtype=jnp.float32)
    inverse = jnp.exp(freq_index * (-2.0 * math.log(rope_base) / HDIM))
    angles = places.astype(jnp.float32)[:, None] * inverse[None, :]
    cosine, sine = jnp.cos(angles), jnp.sin(angles)
    cos_tab = jnp.concatenate([cosine] * 4, axis=1)
    sin_tab = jnp.concatenate([-sine, sine, -sine, sine], axis=1)
    return cos_tab, sin_tab


def mask_columns(seg_rows, live_rows):
    length = seg_rows.shape[0]
    firsts = seg_rows[::TILE]
    same = seg_rows[:, None] == firsts[None, :]
    query_cols = jnp.where(same, 0.0, masked_score)
    key_cols = jnp.where(same, 1.0, 0.0)
    query_cols = jnp.concatenate([query_cols, jnp.ones((length, 1))], axis=1)
    dead = jnp.where(live_rows > 0, 0.0, masked_score)[:, None]
    key_cols = jnp.concatenate([key_cols, dead], axis=1)
    spare = ((0, 0), (0, HDIM - query_cols.shape[1]))
    return (
        jnp.pad(query_cols, spare).astype(jnp.bfloat16),
        jnp.pad(key_cols, spare).astype(jnp.bfloat16),
    )


def swap_halves(values):
    lane = lax.broadcasted_iota(jnp.int32, values.shape, 1)
    return jnp.where(
        lane % HDIM < HDIM // 2,
        pltpu.roll(values, PAIR - HDIM // 2, 1),
        pltpu.roll(values, HDIM // 2, 1),
    )


def rows_dot(left, right):
    return lax.dot_general(left, right, (((1,), (1,)), ((), ())), preferred_element_type=jnp.float32)


def attend_kernel(pq, pk, pv, cos_ref, sin_ref, qm, km, q_out, k_out, v_out, mixed_out, lse_out):
    cos_tab, sin_tab = cos_ref[...], sin_ref[...]
    length = cos_tab.shape[0]
    q_out[...] = ((pq[...] * cos_tab + swap_halves(pq[...]) * sin_tab).astype(jnp.bfloat16)) * 0.125
    k_out[...] = (pk[...] * cos_tab + swap_halves(pk[...]) * sin_tab).astype(jnp.bfloat16)
    v_out[...] = pv[...].astype(jnp.bfloat16)
    flipped = jnp.transpose(v_out[...])
    for begin in range(0, length, QROWS):
        parts = []
        for head in range(PAIR // HDIM):
            cols = slice(head * HDIM, (head + 1) * HDIM)
            keys = jnp.concatenate([k_out[:, cols], km[...]], axis=1)
            rows = jnp.concatenate(
                [q_out[begin : begin + QROWS, cols], qm[begin : begin + QROWS, :]], axis=1
            )
            scores = rows_dot(keys, rows)
            top = jnp.max(scores, axis=0, keepdims=True)
            expo = jnp.exp(scores - top)
            total = jnp.sum(expo, axis=0, keepdims=True)
            lse_out[0, head : head + 1, begin : begin + QROWS] = top + jnp.log(total)
            out = jnp.dot(
                flipped[cols, :], expo.astype(jnp.bfloat16), preferred_element_type=jnp.float32
            )
            parts.append(out / total)
        both = jnp.concatenate(parts, axis=0)
        mixed_out[begin : begin + QROWS, :] = jnp.transpose(both).astype(jnp.bfloat16)


def attend_back_kernel(
    q_ref, k_ref, v_ref, mixed_ref, go_ref, lse_ref, cos_ref, sin_ref, qm, km, gq_out, gk_out, gv_out
):
    cos_tab, sin_tab = cos_ref[...], sin_ref[...]
    length = cos_tab.shape[0]
    product = jnp.transpose(mixed_ref[...].astype(jnp.float32) * go_ref[...].astype(jnp.float32))
    flipped = jnp.transpose(k_ref[...])
    gq_parts, gk_parts, gv_parts = [], [], []
    for head in range(PAIR // HDIM):
        cols = slice(head * HDIM, (head + 1) * HDIM)
        delta = jnp.sum(product[cols, :], axis=0, keepdims=True)
        keys = jnp.concatenate([k_ref[:, cols], km[...]], axis=1)
        values = v_ref[:, cols]
        grad_k = jnp.zeros((length, HDIM), jnp.float32)
        grad_v = jnp.zeros((length, HDIM), jnp.float32)
        grad_q = []
        for begin in range(0, length, QROWS):
            span = slice(begin, begin + QROWS)
            low_q, low_go = q_ref[span, cols], go_ref[span, cols]
            scores = rows_dot(keys, jnp.concatenate([low_q, qm[span, :]], axis=1))
            probs = jnp.exp(scores - lse_ref[0, head : head + 1, span])
            grad_v += jnp.dot(probs.astype(jnp.bfloat16), low_go, preferred_element_type=jnp.float32)
            grad_p = rows_dot(values, low_go)
            grad_s = (probs * (grad_p - delta[:, span])).astype(jnp.bfloat16)
            grad_k += jnp.dot(grad_s, low_q, preferred_element_type=jnp.float32)
            grad_q.append(jnp.dot(flipped[cols, :], grad_s, preferred_element_type=jnp.float32))
        gq_parts.append(jnp.concatenate(grad_q, axis=1))
        gk_parts.append(grad_k)
        gv_parts.append(grad_v)
    grad_q = jnp.transpose(jnp.concatenate(gq_parts, axis=0)) * 0.125
    grad_k = jnp.concatenate(gk_parts, axis=1)
    gq_out[...] = (grad_q * cos_tab + swap_halves(grad_q * sin_tab)).astype(jnp.bfloat16)
    gk_out[...] = (grad_k * cos_tab + swap_halves(grad_k * sin_tab)).astype(jnp.bfloat16)
    gv_out[...] = jnp.concatenate(gv_parts, axis=1).astype(jnp.bfloat16)


def attend(packed, cos_tab, sin_tab, qm, km):
    length, width = packed.shape[0], packed.shape[1] // 3
    pairs = width // PAIR
    block = lambda shift: pl.BlockSpec((length, PAIR), lambda i: (0, i + shift))
    table = pl.BlockSpec((length, PAIR), lambda i: (0, 0))
    mask = pl.BlockSpec((length, HDIM), lambda i: (0, 0))
    rows = jax.ShapeDtypeStruct((length, width), jnp.bfloat16)
    return pl.pallas_call(
        attend_kernel,
        grid=(pairs,),
        in_specs=[block(0), block(pairs), block(2 * pairs), table, table, mask, mask],
        out_specs=[block(0)] * 4 + [pl.BlockSpec((1, 2, length), lambda i: (i, 0, 0))],
        out_shape=[rows] * 4 + [jax.ShapeDtypeStruct((pairs, 2, length), jnp.float32)],
        compiler_params=pltpu.CompilerParams(vmem_limit_bytes=40 << 20),
        cost_estimate=pl.CostEstimate(
            flops=16 * width * length * length, bytes_accessed=20 * length * width,
            transcendentals=pairs * 2 * length * length,
        ),
    )(packed, packed, packed, cos_tab, sin_tab, qm, km)


def attend_back(queries, keyset, valueset, mixed, grad_mixed, lse, cos_tab, sin_tab, qm, km):
    length, width = queries.shape
    pairs = width // PAIR
    block = pl.BlockSpec((length, PAIR), lambda i: (0, i))
    table = pl.BlockSpec((length, PAIR), lambda i: (0, 0))
    mask = pl.BlockSpec((length, HDIM), lambda i: (0, 0))
    rows = jax.ShapeDtypeStruct((length, width), jnp.bfloat16)
    return pl.pallas_call(
        attend_back_kernel,
        grid=(pairs,),
        in_specs=[block] * 5
        + [pl.BlockSpec((1, 2, length), lambda i: (i, 0, 0)), table, table, mask, mask],
        out_specs=[block] * 3,
        out_shape=[rows] * 3,
        compiler_params=pltpu.CompilerParams(vmem_limit_bytes=48 << 20),
        cost_estimate=pl.CostEstimate(
            flops=40 * width * length * length, bytes_accessed=16 * length * width,
            transcendentals=pairs * 2 * length * length,
        ),
    )(queries, keyset, valueset, mixed, grad_mixed, lse, cos_tab, sin_tab, qm, km)


def swap_with(array, axis, bit):
    size = lax.axis_size(axis)
    return lax.ppermute(array, axis, [(i, i ^ (1 << bit)) for i in range(size)])


def side_of(axis, bit):
    return (lax.axis_index(axis) >> bit) & 1


def bits_of(axis):
    return [(axis, bit) for bit in reversed(range(lax.axis_size(axis).bit_length() - 1))]


def gather_half(piece, order):
    canon = bits_of("fsdp") + bits_of("rep")
    have = []
    for axis, bit in order:
        other = swap_with(piece, axis, bit)
        side = side_of(axis, bit) == 0
        place = sum(canon.index(known) < canon.index((axis, bit)) for known in have)
        piece = jnp.stack(
            [jnp.where(side, piece, other), jnp.where(side, other, piece)], axis=place
        )
        have.append((axis, bit))
    return piece.reshape(-1, piece.shape[-1])


def pick(array, dim, side):
    return lax.dynamic_index_in_dim(array, side, dim, keepdims=False)


def orders():
    rep_bits, fsdp_bits = bits_of("rep")[::-1], bits_of("fsdp")[::-1]
    near, far = rep_bits[0], rep_bits[1:]
    one = [near] + far + fsdp_bits
    two = [near] + fsdp_bits[:1] + far + fsdp_bits[1:]
    return one, two


def gather_weights(arrays):
    joint = jnp.concatenate(arrays, axis=1)
    for axis, bit in bits_of("rep"):
        size = joint.shape[0] // 2
        joint = lax.dynamic_slice_in_dim(joint, side_of(axis, bit) * size, size, axis=0)
    cut = joint.shape[1] // 256 * 128
    one, two = orders()
    whole = jnp.concatenate(
        [gather_half(joint[:, :cut], one[::-1]), gather_half(joint[:, cut:], two[::-1])], axis=1
    )
    outs, start = [], 0
    for array in arrays:
        outs.append(whole[:, start : start + array.shape[1]])
        start += array.shape[1]
    return outs


def scatter_half(term, order):
    canon = bits_of("fsdp") + bits_of("rep")
    rows = term.shape[0] >> len(canon)
    acc = term.reshape([2] * len(canon) + [rows, term.shape[1]])
    left = list(canon)
    for axis, bit in order:
        dim = left.index((axis, bit))
        side = side_of(axis, bit)
        other = swap_with(pick(acc, dim, 1 - side), axis, bit)
        acc = pick(acc, dim, side).astype(jnp.float32) + other.astype(jnp.float32)
        acc = acc.astype(jnp.bfloat16)
        left.remove((axis, bit))
    rep_order = [entry for entry in order[::-1] if entry[0] == "rep"]
    have = []
    for axis, bit in rep_order:
        other = swap_with(acc, axis, bit)
        side = side_of(axis, bit) == 0
        place = sum(canon.index(known) < canon.index((axis, bit)) for known in have)
        acc = jnp.stack([jnp.where(side, acc, other), jnp.where(side, other, acc)], axis=place)
        have.append((axis, bit))
    return acc.reshape(-1, acc.shape[-1]).astype(jnp.float32)


def scatter_sums(terms):
    joint = jnp.concatenate([term.astype(jnp.bfloat16) for term in terms], axis=1)
    cut = joint.shape[1] // 256 * 128
    one, two = orders()
    whole = jnp.concatenate(
        [scatter_half(joint[:, :cut], one), scatter_half(joint[:, cut:], two)], axis=1
    )
    outs, start = [], 0
    for term in terms:
        outs.append(whole[:, start : start + term.shape[1]])
        start += term.shape[1]
    return outs


def geglu(lifted):
    half_ff = lifted.shape[1] // 2
    return jax.nn.gelu(lifted[:, :half_ff], approximate=False) * lifted[:, half_ff:]


def on_device(
    layer_input,
    qkv_weight,
    attn_weight,
    wide_weight,
    narrow_weight,
    first_gain,
    second_gain,
    out_grad,
    token_seg,
    token_live,
):
    gains = jnp.stack([first_gain, second_gain], axis=1)
    gains = jnp.pad(gains, ((0, 0), (0, PAIR - 2)))
    qkv_full, gains = gather_weights([qkv_weight, gains])
    attn_full, wide_full, narrow_full = gather_weights([attn_weight, wide_weight, narrow_weight])
    scale_one = gains[:, 0].astype(jnp.float32)
    scale_two = gains[:, 1].astype(jnp.float32)
    residual_in = layer_input.astype(jnp.float32)
    qm, km = mask_columns(token_seg, token_live)
    cos_tab, sin_tab = rope_tables(token_seg)
    normed_one = layer_norm(residual_in, scale_one).astype(jnp.bfloat16)
    packed = jnp.dot(normed_one, qkv_full, preferred_element_type=jnp.float32)
    queries, keyset, valueset, mixed_rows, lse = attend(packed, cos_tab, sin_tab, qm, km)
    middle = residual_in + jnp.dot(mixed_rows, attn_full, preferred_element_type=jnp.float32)
    normed_two = layer_norm(middle, scale_two).astype(jnp.bfloat16)
    lifted = jnp.dot(normed_two, wide_full, preferred_element_type=jnp.float32)
    hidden = geglu(lifted).astype(jnp.bfloat16)
    layer_out = middle + jnp.einsum(
        "tf,df->td", hidden, narrow_full, preferred_element_type=jnp.float32
    )
    grad_top = out_grad.astype(jnp.float32) * token_live.astype(jnp.float32)[:, None]
    grad_top_low = grad_top.astype(jnp.bfloat16)
    narrow_term = jnp.einsum("td,tf->df", grad_top_low, hidden, preferred_element_type=jnp.float32)
    grad_hidden = jnp.dot(grad_top_low, narrow_full, preferred_element_type=jnp.float32)
    _, pull_gate = jax.vjp(geglu, lifted)
    grad_lifted = pull_gate(grad_hidden)[0].astype(jnp.bfloat16)
    wide_term = jnp.einsum("td,tf->df", normed_two, grad_lifted, preferred_element_type=jnp.float32)
    grad_norm_two = jnp.einsum(
        "tf,df->td", grad_lifted, wide_full, preferred_element_type=jnp.float32
    )
    _, pull_two = jax.vjp(layer_norm, middle, scale_two)
    grad_mid_ln, second_term = pull_two(grad_norm_two)
    grad_middle = grad_top + grad_mid_ln
    grad_middle_low = grad_middle.astype(jnp.bfloat16)
    attn_term = jnp.einsum(
        "td,te->de", mixed_rows, grad_middle_low, preferred_element_type=jnp.float32
    )
    grad_mixed = jnp.einsum(
        "te,de->td", grad_middle_low, attn_full, preferred_element_type=jnp.float32
    )
    shares = scatter_sums([narrow_term, wide_term, attn_term])
    grad_parts = attend_back(
        queries, keyset, valueset, mixed_rows, grad_mixed.astype(jnp.bfloat16), lse,
        cos_tab, sin_tab, qm, km,
    )
    grad_packed = jnp.concatenate(grad_parts, axis=1)
    qkv_term = jnp.einsum("td,tf->df", normed_one, grad_packed, preferred_element_type=jnp.float32)
    grad_norm_one = jnp.einsum(
        "tf,df->td", grad_packed, qkv_full, preferred_element_type=jnp.float32
    )
    _, pull_one = jax.vjp(layer_norm, residual_in, scale_one)
    grad_in_ln, first_term = pull_one(grad_norm_one)
    input_grad = grad_middle + grad_in_ln
    gain_terms = jnp.stack([first_term, second_term], axis=1)
    gain_terms = jnp.pad(gain_terms, ((0, 0), (0, PAIR - 2)))
    qkv_share, gain_share = scatter_sums([qkv_term, gain_terms])
    return (
        layer_out.astype(jnp.bfloat16),
        input_grad,
        qkv_share,
        shares[2],
        shares[1],
        shares[0],
        gain_share[:, 0],
        gain_share[:, 1],
    )


def solution(mesh):
    return jax.shard_map(
        on_device,
        mesh=mesh,
        in_specs=(
            P(("fsdp", "rep"), None),
            P("fsdp", None),
            P("fsdp", None),
            P("fsdp", None),
            P("fsdp", None),
            P("fsdp"),
            P("fsdp"),
            P(("fsdp", "rep"), None),
            P(("fsdp", "rep")),
            P(("fsdp", "rep")),
        ),
        out_specs=(
            P(("fsdp", "rep"), None),
            P(("fsdp", "rep"), None),
            P("fsdp", None),
            P("fsdp", None),
            P("fsdp", None),
            P("fsdp", None),
            P("fsdp"),
            P("fsdp"),
        ),
        check_vma=False,
    )
```

```python
import math

import jax
import jax.numpy as jnp
from jax import lax
from jax.experimental import pallas as pl
from jax.experimental.pallas import tpu as pltpu
from jax.sharding import PartitionSpec as P

HDIM = 64
TILE = 128
PAIR = 128
QROWS = 256


rope_base = 160000.0
eps = 1e-05
masked_score = -1e30


def layer_norm(values, scales):
    center = values - jnp.mean(values, axis=-1, keepdims=True)
    spread = jnp.mean(center * center, axis=-1, keepdims=True)
    return center * lax.rsqrt(spread + eps) * scales


def rope_tables(seg_rows):
    length = seg_rows.shape[0]
    firsts = seg_rows[::TILE]
    before = jnp.sum((firsts[None, :] < seg_rows[:, None]).astype(jnp.int32), axis=1)
    places = jnp.arange(length, dtype=jnp.int32) - TILE * before
    freq_index = jnp.arange(HDIM // 2, dtype=jnp.float32)
    inverse = jnp.exp(freq_index * (-2.0 * math.log(rope_base) / HDIM))
    angles = places.astype(jnp.float32)[:, None] * inverse[None, :]
    cosine, sine = jnp.cos(angles), jnp.sin(angles)
    cos_tab = jnp.concatenate([cosine] * 4, axis=1)
    sin_tab = jnp.concatenate([-sine, sine, -sine, sine], axis=1)
    return cos_tab, sin_tab


def mask_columns(seg_rows, live_rows):
    length = seg_rows.shape[0]
    firsts = seg_rows[::TILE]
    same = seg_rows[:, None] == firsts[None, :]
    query_cols = jnp.where(same, 0.0, masked_score)
    key_cols = jnp.where(same, 1.0, 0.0)
    query_cols = jnp.concatenate([query_cols, jnp.ones((length, 1))], axis=1)
    dead = jnp.where(live_rows > 0, 0.0, masked_score)[:, None]
    key_cols = jnp.concatenate([key_cols, dead], axis=1)
    spare = ((0, 0), (0, HDIM - query_cols.shape[1]))
    return (
        jnp.pad(query_cols, spare).astype(jnp.bfloat16),
        jnp.pad(key_cols, spare).astype(jnp.bfloat16),
    )


def swap_halves(values):
    lane = lax.broadcasted_iota(jnp.int32, values.shape, 1)
    return jnp.where(
        lane % HDIM < HDIM // 2,
        pltpu.roll(values, PAIR - HDIM // 2, 1),
        pltpu.roll(values, HDIM // 2, 1),
    )


def rows_dot(left, right):
    return lax.dot_general(left, right, (((1,), (1,)), ((), ())), preferred_element_type=jnp.float32)


def attend_kernel(pq, pk, pv, cos_ref, sin_ref, qm, km, q_out, k_out, v_out, mixed_out, lse_out):
    cos_tab, sin_tab = cos_ref[...], sin_ref[...]
    length = cos_tab.shape[0]
    q_out[...] = ((pq[...] * cos_tab + swap_halves(pq[...]) * sin_tab).astype(jnp.bfloat16)) * 0.125
    k_out[...] = (pk[...] * cos_tab + swap_halves(pk[...]) * sin_tab).astype(jnp.bfloat16)
    v_out[...] = pv[...].astype(jnp.bfloat16)
    flipped = jnp.transpose(pv[...].astype(jnp.bfloat16))
    low_q, low_k = q_out[...], k_out[...]
    parts, lse_parts = [], []
    for head in range(PAIR // HDIM):
        cols = slice(head * HDIM, (head + 1) * HDIM)
        keys = jnp.concatenate([low_k[:, cols], km[...]], axis=1)
        rows = jnp.concatenate([low_q[:, cols], qm[...]], axis=1)
        pieces, lse_pieces = [], []
        for begin in range(0, length, QROWS):
            scores = rows_dot(keys, rows[begin : begin + QROWS])
            top = jnp.max(scores, axis=0, keepdims=True)
            expo = jnp.exp(scores - top)
            total = jnp.sum(expo, axis=0, keepdims=True)
            out = jnp.dot(
                flipped[cols, :], expo.astype(jnp.bfloat16), preferred_element_type=jnp.float32
            )
            pieces.append(out / total)
            lse_pieces.append(top + jnp.log(total))
        parts.append(jnp.concatenate(pieces, axis=1))
        lse_parts.append(jnp.concatenate(lse_pieces, axis=1))
    mixed_out[...] = jnp.transpose(jnp.concatenate(parts, axis=0)).astype(jnp.bfloat16)
    lse_out[0, :, :] = jnp.concatenate(lse_parts, axis=0)


def attend_back_kernel(
    q_ref, k_ref, v_ref, mixed_ref, go_ref, lse_ref, cos_ref, sin_ref, qm, km, gq_out, gk_out, gv_out
):
    cos_tab, sin_tab = cos_ref[...], sin_ref[...]
    length = cos_tab.shape[0]
    product = jnp.transpose(mixed_ref[...].astype(jnp.float32) * go_ref[...].astype(jnp.float32))
    flipped = jnp.transpose(k_ref[...])
    gq_parts, gk_parts, gv_parts = [], [], []
    for head in range(PAIR // HDIM):
        cols = slice(head * HDIM, (head + 1) * HDIM)
        delta = jnp.sum(product[cols, :], axis=0, keepdims=True)
        keys = jnp.concatenate([k_ref[:, cols], km[...]], axis=1)
        values = v_ref[:, cols]
        grad_k = jnp.zeros((length, HDIM), jnp.float32)
        grad_v = jnp.zeros((length, HDIM), jnp.float32)
        grad_q = []
        for begin in range(0, length, QROWS):
            span = slice(begin, begin + QROWS)
            low_q, low_go = q_ref[span, cols], go_ref[span, cols]
            scores = rows_dot(keys, jnp.concatenate([low_q, qm[span, :]], axis=1))
            probs = jnp.exp(scores - lse_ref[0, head : head + 1, span])
            grad_v += jnp.dot(probs.astype(jnp.bfloat16), low_go, preferred_element_type=jnp.float32)
            grad_p = rows_dot(values, low_go)
            grad_s = (probs * (grad_p - delta[:, span])).astype(jnp.bfloat16)
            grad_k += jnp.dot(grad_s, low_q, preferred_element_type=jnp.float32)
            grad_q.append(jnp.dot(flipped[cols, :], grad_s, preferred_element_type=jnp.float32))
        gq_parts.append(jnp.concatenate(grad_q, axis=1))
        gk_parts.append(grad_k)
        gv_parts.append(grad_v)
    grad_q = jnp.transpose(jnp.concatenate(gq_parts, axis=0)) * 0.125
    grad_k = jnp.concatenate(gk_parts, axis=1)
    gq_out[...] = (grad_q * cos_tab + swap_halves(grad_q * sin_tab)).astype(jnp.bfloat16)
    gk_out[...] = (grad_k * cos_tab + swap_halves(grad_k * sin_tab)).astype(jnp.bfloat16)
    gv_out[...] = jnp.concatenate(gv_parts, axis=1).astype(jnp.bfloat16)


def attend(packed, cos_tab, sin_tab, qm, km, first, count):
    length, all_pairs = packed.shape[0], packed.shape[1] // (3 * PAIR)
    block = lambda shift: pl.BlockSpec((length, PAIR), lambda i: (0, i + shift))
    table = pl.BlockSpec((length, PAIR), lambda i: (0, 0))
    mask = pl.BlockSpec((length, HDIM), lambda i: (0, 0))
    rows = jax.ShapeDtypeStruct((length, count * PAIR), jnp.bfloat16)
    return pl.pallas_call(
        attend_kernel,
        grid=(count,),
        in_specs=[block(first), block(first + all_pairs), block(first + 2 * all_pairs)]
        + [table, table, mask, mask],
        out_specs=[block(0)] * 4 + [pl.BlockSpec((1, 2, length), lambda i: (i, 0, 0))],
        out_shape=[rows] * 4 + [jax.ShapeDtypeStruct((count, 2, length), jnp.float32)],
        compiler_params=pltpu.CompilerParams(vmem_limit_bytes=40 << 20),
        cost_estimate=pl.CostEstimate(
            flops=6400 * count * length * length, bytes_accessed=20 * length * PAIR * count,
            transcendentals=count * 2 * length * length,
        ),
    )(packed, packed, packed, cos_tab, sin_tab, qm, km)


def attend_back(queries, keyset, valueset, mixed, grad_mixed, lse, tables, first):
    length, count = queries.shape[0], queries.shape[1] // PAIR
    block = pl.BlockSpec((length, PAIR), lambda i: (0, i))
    later = pl.BlockSpec((length, PAIR), lambda i: (0, i + first))
    table = pl.BlockSpec((length, PAIR), lambda i: (0, 0))
    mask = pl.BlockSpec((length, HDIM), lambda i: (0, 0))
    rows = jax.ShapeDtypeStruct((length, count * PAIR), jnp.bfloat16)
    return pl.pallas_call(
        attend_back_kernel,
        grid=(count,),
        in_specs=[block] * 4
        + [later, pl.BlockSpec((1, 2, length), lambda i: (i, 0, 0)), table, table, mask, mask],
        out_specs=[block] * 3,
        out_shape=[rows] * 3,
        compiler_params=pltpu.CompilerParams(vmem_limit_bytes=48 << 20),
        cost_estimate=pl.CostEstimate(
            flops=6400 * count * length * length, bytes_accessed=16 * length * PAIR * count,
            transcendentals=count * 2 * length * length,
        ),
    )(queries, keyset, valueset, mixed, grad_mixed, lse, *tables)


def swap_with(array, axis, bit):
    size = lax.axis_size(axis)
    return lax.ppermute(array, axis, [(i, i ^ (1 << bit)) for i in range(size)])


def side_of(axis, bit):
    return (lax.axis_index(axis) >> bit) & 1


def bits_of(axis):
    return [(axis, bit) for bit in reversed(range(lax.axis_size(axis).bit_length() - 1))]


class Gather:
    def __init__(self, arrays, order):
        self.widths = [array.shape[1] for array in arrays]
        joint = jnp.concatenate(arrays, axis=1) if len(arrays) > 1 else arrays[0]
        for axis, bit in bits_of("rep"):
            size = joint.shape[0] // 2
            joint = lax.dynamic_slice_in_dim(joint, side_of(axis, bit) * size, size, axis=0)
        self.value, self.order, self.have = joint, list(order), []

    def step(self):
        canon = bits_of("fsdp") + bits_of("rep")
        axis, bit = self.order.pop(0)
        other = swap_with(self.value, axis, bit)
        side = side_of(axis, bit) == 0
        place = sum(canon.index(known) < canon.index((axis, bit)) for known in self.have)
        self.value = jnp.stack(
            [jnp.where(side, self.value, other), jnp.where(side, other, self.value)], axis=place
        )
        self.have.append((axis, bit))

    def finish(self):
        while self.order:
            self.step()
        whole = self.value.reshape(-1, self.value.shape[-1])
        outs, start = [], 0
        for width in self.widths:
            outs.append(whole[:, start : start + width])
            start += width
        return outs


def pick(array, dim, side):
    return lax.dynamic_index_in_dim(array, side, dim, keepdims=False)


def orders():
    rep_bits, fsdp_bits = bits_of("rep")[::-1], bits_of("fsdp")[::-1]
    near, far = rep_bits[0], rep_bits[1:]
    one = [near] + far + fsdp_bits
    two = [near] + fsdp_bits[:1] + far + fsdp_bits[1:]
    return one, two


class Scatter:
    def __init__(self, terms, order):
        self.widths = [term.shape[1] for term in terms]
        terms = [term.astype(jnp.bfloat16) for term in terms]
        term = jnp.concatenate(terms, axis=1) if len(terms) > 1 else terms[0]
        canon = bits_of("fsdp") + bits_of("rep")
        rows = term.shape[0] >> len(canon)
        self.value = term.reshape([2] * len(canon) + [rows, term.shape[1]])
        self.left, self.order, self.have = canon, list(order), []
        self.joins = [entry for entry in order[::-1] if entry[0] == "rep"]

    def step(self):
        if self.order:
            axis, bit = self.order.pop(0)
            dim = self.left.index((axis, bit))
            side = side_of(axis, bit)
            other = swap_with(pick(self.value, dim, 1 - side), axis, bit)
            total = pick(self.value, dim, side).astype(jnp.float32) + other.astype(jnp.float32)
            self.value = total.astype(jnp.bfloat16)
            self.left.remove((axis, bit))
        elif self.joins:
            canon = bits_of("rep")
            axis, bit = self.joins.pop(0)
            other = swap_with(self.value, axis, bit)
            side = side_of(axis, bit) == 0
            place = sum(canon.index(known) < canon.index((axis, bit)) for known in self.have)
            self.value = jnp.stack(
                [jnp.where(side, self.value, other), jnp.where(side, other, self.value)], axis=place
            )
            self.have.append((axis, bit))

    def finish(self):
        while self.order or self.joins:
            self.step()
        whole = self.value.reshape(-1, self.value.shape[-1]).astype(jnp.float32)
        outs, start = [], 0
        for width in self.widths:
            outs.append(whole[:, start : start + width])
            start += width
        return outs


def advance(chains, values, steps=1):
    held = lax.optimization_barrier((tuple(chain.value for chain in chains), values))
    for chain, value in zip(chains, held[0]):
        chain.value = value
        for _ in range(steps):
            chain.step()
    return held[1]


def geglu(lifted):
    half_ff = lifted.shape[1] // 2
    return jax.nn.gelu(lifted[:, :half_ff], approximate=False) * lifted[:, half_ff:]


def on_device(
    layer_input,
    qkv_weight,
    attn_weight,
    wide_weight,
    narrow_weight,
    first_gain,
    second_gain,
    out_grad,
    token_seg,
    token_live,
):
    gains = jnp.stack([first_gain, second_gain], axis=1)
    gains = jnp.pad(gains, ((0, 0), (0, PAIR - 2)))
    one, two = orders()
    half = qkv_weight.shape[1] // 256 * 128
    left = Gather([qkv_weight[:, :half]], one[::-1])
    right = Gather([qkv_weight[:, half:], gains], two[::-1])
    for _ in range(len(one) - 2):
        left.step()
        right.step()
    upper = Gather([attn_weight, narrow_weight], one[::-1])
    lower = Gather([wide_weight], two[::-1])
    left.value, right.value = advance([upper, lower], (left.value, right.value))
    (qkv_left,) = left.finish()
    qkv_right, gains = right.finish()
    qkv_full = jnp.concatenate([qkv_left, qkv_right], axis=1)
    scale_one = gains[:, 0].astype(jnp.float32)
    scale_two = gains[:, 1].astype(jnp.float32)
    residual_in = layer_input.astype(jnp.float32)
    qm, km = mask_columns(token_seg, token_live)
    cos_tab, sin_tab = rope_tables(token_seg)
    normed_one = layer_norm(residual_in, scale_one).astype(jnp.bfloat16)
    packed = jnp.dot(normed_one, qkv_full, preferred_element_type=jnp.float32)
    pairs = packed.shape[1] // (3 * PAIR)
    count = pairs // 3 if pairs % 3 == 0 else pairs
    tables = (cos_tab, sin_tab, qm, km)
    attended = []
    for first in range(0, pairs, count):
        if attended:
            packed, _ = advance([upper, lower], (packed, attended[-1]))
        else:
            packed = advance([upper, lower], packed)
        attended.append(attend(packed, *tables, first, count))
    mixed_rows = jnp.concatenate([group[3] for group in attended], axis=1)
    attn_full, narrow_full = upper.finish()
    (wide_full,) = lower.finish()
    middle = residual_in + jnp.dot(mixed_rows, attn_full, preferred_element_type=jnp.float32)
    normed_two = layer_norm(middle, scale_two).astype(jnp.bfloat16)
    lifted = jnp.dot(normed_two, wide_full, preferred_element_type=jnp.float32)
    hidden = geglu(lifted).astype(jnp.bfloat16)
    layer_out = middle + jnp.einsum(
        "tf,df->td", hidden, narrow_full, preferred_element_type=jnp.float32
    )
    grad_top = out_grad.astype(jnp.float32) * token_live.astype(jnp.float32)[:, None]
    grad_top_low = grad_top.astype(jnp.bfloat16)
    narrow_term = jnp.einsum("td,tf->df", grad_top_low, hidden, preferred_element_type=jnp.float32)
    grad_hidden = jnp.dot(grad_top_low, narrow_full, preferred_element_type=jnp.float32)
    _, pull_gate = jax.vjp(geglu, lifted)
    grad_lifted = pull_gate(grad_hidden)[0].astype(jnp.bfloat16)
    wide_term = jnp.einsum("td,tf->df", normed_two, grad_lifted, preferred_element_type=jnp.float32)
    wide_sum, narrow_sum = Scatter([wide_term], one), Scatter([narrow_term], two)
    grad_lifted = advance([wide_sum, narrow_sum], grad_lifted)
    grad_norm_two = jnp.einsum(
        "tf,df->td", grad_lifted, wide_full, preferred_element_type=jnp.float32
    )
    _, pull_two = jax.vjp(layer_norm, middle, scale_two)
    grad_mid_ln, second_term = pull_two(grad_norm_two)
    grad_middle = grad_top + grad_mid_ln
    grad_middle_low = grad_middle.astype(jnp.bfloat16)
    attn_term = jnp.einsum(
        "td,te->de", mixed_rows, grad_middle_low, preferred_element_type=jnp.float32
    )
    grad_mixed = jnp.einsum(
        "te,de->td", grad_middle_low, attn_full, preferred_element_type=jnp.float32
    )
    grad_mixed = grad_mixed.astype(jnp.bfloat16)
    chains, grad_groups, qkv_sums = [wide_sum, narrow_sum], [], []
    for index, group in enumerate(attended):
        if grad_groups:
            group_grad = jnp.concatenate(grad_groups[-1], axis=1)
            term = jnp.einsum("td,tf->df", normed_one, group_grad, preferred_element_type=jnp.float32)
            terms = [term] if qkv_sums else [term, attn_term]
            qkv_sums.append(Scatter(terms, one if len(qkv_sums) % 2 else two))
            chains.append(qkv_sums[-1])
        grad_mixed = advance(chains, grad_mixed)
        queries, keyset, valueset, mixed, lse = group
        grad_group = attend_back(
            queries, keyset, valueset, mixed, grad_mixed, lse, tables, index * count
        )
        grad_groups.append(advance(chains, grad_group, 0))
    group_grad = jnp.concatenate(grad_groups[-1], axis=1)
    term = jnp.einsum("td,tf->df", normed_one, group_grad, preferred_element_type=jnp.float32)
    grad_packed = jnp.concatenate([group[kind] for kind in range(3) for group in grad_groups], axis=1)
    grad_packed = advance(chains, grad_packed)
    grad_norm_one = jnp.einsum(
        "tf,df->td", grad_packed, qkv_full, preferred_element_type=jnp.float32
    )
    _, pull_one = jax.vjp(layer_norm, residual_in, scale_one)
    grad_in_ln, first_term = pull_one(grad_norm_one)
    input_grad = grad_middle + grad_in_ln
    gain_terms = jnp.stack([first_term, second_term], axis=1)
    gain_terms = jnp.pad(gain_terms, ((0, 0), (0, PAIR - 2)))
    cut = count * PAIR
    early = [term] if qkv_sums else [term, attn_term]
    qkv_sums.append(Scatter(early + [gain_terms], one))
    finished = [chain.finish() for chain in qkv_sums]
    pieces = [outs[0] for outs in finished]
    attn_share, gain_share = finished[0][1], finished[-1][-1]
    qkv_share = jnp.concatenate(
        [piece[:, kind * cut : (kind + 1) * cut] for kind in range(3) for piece in pieces], axis=1
    )
    (wide_share,) = wide_sum.finish()
    (narrow_share,) = narrow_sum.finish()
    return (
        layer_out.astype(jnp.bfloat16),
        input_grad,
        qkv_share,
        attn_share,
        wide_share,
        narrow_share,
        gain_share[:, 0],
        gain_share[:, 1],
    )


def solution(mesh):
    return jax.shard_map(
        on_device,
        mesh=mesh,
        in_specs=(
            P(("fsdp", "rep"), None),
            P("fsdp", None),
            P("fsdp", None),
            P("fsdp", None),
            P("fsdp", None),
            P("fsdp"),
            P("fsdp"),
            P(("fsdp", "rep"), None),
            P(("fsdp", "rep")),
            P(("fsdp", "rep")),
        ),
        out_specs=(
            P(("fsdp", "rep"), None),
            P(("fsdp", "rep"), None),
            P("fsdp", None),
            P("fsdp", None),
            P("fsdp", None),
            P("fsdp", None),
            P("fsdp"),
            P("fsdp"),
        ),
        check_vma=False,
    )
```
